256 devices in a mesh: row: 8 (over y, x_hi), col: 32 (over x_lo, z, core).
Axes of the slice: x: 4 (x_hi: 2, x_lo: 2; x = x_hi * 2 + x_lo), y: 4, z: 8, core: 2. Of those that a mesh axis runs over, the one named last changes fastest.
Arguments:
- tokens: bfloat16 [512, 12288], P('col', 'row'), may hold values from -6 to 6
- up_weight: bfloat16 [12288, 24576], P('row', 'col'), may hold values from -0.0546875 to 0.0546875
- up_bias: bfloat16 [24576], P('col'), may hold values from -4 to 4
- down_weight: bfloat16 [24576, 12288], P('col', 'row'), may hold values from -0.0390625 to 0.0390625
- cotangent: bfloat16 [512, 12288], P('col', 'row'), may hold values from -6 to 6
Outputs:
- grad_tokens: bfloat16 [512, 12288], P('col', 'row')
- grad_up: bfloat16 [12288, 24576], P('row', 'col')
- grad_down: bfloat16 [24576, 12288], P('col', 'row')
The draws below stay inside these ranges and needn't reach their ends.
All inputs are finite; a program needn't handle non-finite values.
Results may differ from the reference program's by a relative error of at most 0.0049.
Values may be sent and summed in bfloat16 or wider, within the bound.
No kernel may reach another device: no remote copies, remote signals or barrier semaphores. Data moves between devices by JAX's collectives and lax.ppermute only.
A program may use at most 64 MiB of HBM per device.

```python
import math
import jax
import jax.numpy as jnp
from jax import lax

D = 12288
FF = 24576
TOKENS = 512


def steps_of(own_key, extent, shards, low, top_value):
    def one(dim, shards_of):
        steps = jax.random.uniform(jax.random.fold_in(jax.random.fold_in(own_key, 6), dim), (shards_of,), jnp.float32, low / len(shards), top_value / len(shards))
        return jnp.repeat(jnp.exp(steps), extent[dim] // shards_of).reshape((-1,) + (1,) * (len(extent) - dim - 1))

    level = one(*shards[0])
    for cut in shards[1:]:
        level = level * one(*cut)
    return level


def centred(key, extent, scale, reach, split=(), kind=jnp.bfloat16):
    gain = steps_of(key, extent, split, -0.22, 0.18) if split else 1.0
    values = jax.random.normal(key, extent, jnp.float32) * scale * gain
    return jnp.minimum(jnp.maximum(values, -reach), reach).astype(kind)


def setup_inputs(seed: int = 0) -> dict:
    splits = jax.random.split(jax.random.key(seed), 6)
    return {
        "tokens": centred(splits[0], (TOKENS, D), 1.0, 6.0, ((0, 32), (1, 8))),
        "up_weight": centred(splits[1], (D, FF), D ** -0.5, 0.0546875, ((0, 8), (1, 32))),
        "up_bias": centred(splits[2], (FF,), 1.0, 4.0, ((0, 32),)),
        "down_weight": centred(splits[3], (FF, D), FF ** -0.5, 0.0390625, ((0, 32), (1, 8))),
        "cotangent": centred(splits[4], (TOKENS, D), 1.0, 6.0, ((0, 32), (1, 8))),
    }


def gelu_value(hidden):
    return hidden * 0.5 * (1.0 + lax.erf(hidden / math.sqrt(2.0)))

def gelu_slope(hidden):
    cumulative = 0.5 * (1.0 + lax.erf(hidden / math.sqrt(2.0)))
    density = jnp.exp(-0.5 * hidden * hidden) / math.sqrt(2.0 * math.pi)
    return cumulative + hidden * density

def reference(tokens, up_weight, up_bias, down_weight, cotangent):
    hidden = jnp.dot(tokens, up_weight, preferred_element_type=jnp.float32) + up_bias.astype(jnp.float32)
    activated = gelu_value(hidden).astype(jnp.bfloat16)
    act_grad = lax.dot_general(cotangent, down_weight, (((1,), (1,)), ((), ())), preferred_element_type=jnp.float32)
    hidden_grad = (act_grad * gelu_slope(hidden)).astype(jnp.bfloat16)
    grad_tokens = lax.dot_general(hidden_grad, up_weight, (((1,), (1,)), ((), ())), preferred_element_type=jnp.float32)
    norm_factor = 1.0 / math.sqrt(TOKENS)
    grad_up = lax.dot_general(tokens, hidden_grad, (((0,), (0,)), ((), ())), preferred_element_type=jnp.float32) * norm_factor
    grad_down = lax.dot_general(activated, cotangent, (((0,), (0,)), ((), ())), preferred_element_type=jnp.float32) * norm_factor
    return (grad_tokens.astype(jnp.bfloat16), grad_up.astype(jnp.bfloat16), grad_down.astype(jnp.bfloat16))
```

```python
import math

import jax
import jax.numpy as jnp
from jax import lax
from jax.sharding import Mesh, PartitionSpec as P

ROW = ("y", "x_hi")
COL = ("x_lo", "z", "core")
BF16 = jnp.bfloat16
F32 = jnp.float32


def gelu_value(hidden):
    return hidden * 0.5 * (1.0 + lax.erf(hidden / math.sqrt(2.0)))


def gelu_slope(hidden):
    cumulative = 0.5 * (1.0 + lax.erf(hidden / math.sqrt(2.0)))
    density = jnp.exp(-0.5 * hidden * hidden) / math.sqrt(2.0 * math.pi)
    return cumulative + hidden * density


def pointwise(hidden_sum, act_grad, up_bias):
    hidden = hidden_sum + up_bias.astype(F32)[None, :]
    activated = gelu_value(hidden).astype(BF16)
    hidden_grad = (act_grad * gelu_slope(hidden)).astype(BF16)
    return (activated, hidden_grad)


def on_device(tokens, up_weight, up_bias, down_weight, cotangent):
    width, units = up_weight.shape
    packed = jnp.concatenate([tokens, cotangent], axis=1)
    gathered = lax.all_gather(packed, COL, axis=0, tiled=True)
    all_rows, all_cots = gathered[:, :width], gathered[:, width:]
    count = all_rows.shape[0]
    hidden_part = jnp.dot(all_rows, up_weight, preferred_element_type=F32).astype(BF16)
    act_part = lax.dot_general(
        all_cots, down_weight, (((1,), (1,)), ((), ())), preferred_element_type=F32
    ).astype(BF16)
    parts = jnp.concatenate([hidden_part, act_part], axis=1)
    parts = lax.all_to_all(parts, ROW, 0, 0, tiled=True)
    sums = parts.reshape(8, count // 8, 2 * units).astype(F32).sum(axis=0)
    activated, hidden_grad = pointwise(sums[:, :units], sums[:, units:], up_bias)
    both = jnp.concatenate([activated, hidden_grad], axis=1)
    both = lax.all_to_all(jnp.tile(both, (8, 1)), ROW, 0, 0, tiled=True)
    activated, hidden_grad = both[:, :units], both[:, units:]
    norm_factor = 1.0 / math.sqrt(count)
    token_part = lax.dot_general(
        hidden_grad, up_weight, (((1,), (1,)), ((), ())), preferred_element_type=F32
    ).astype(BF16)
    token_part = lax.all_to_all(token_part, COL, 0, 0, tiled=True)
    grad_tokens = token_part.reshape(32, count // 32, width).astype(F32).sum(axis=0)
    grad_up = (
        lax.dot_general(
            all_rows, hidden_grad, (((0,), (0,)), ((), ())), preferred_element_type=F32
        )
        * norm_factor
    )
    grad_down = (
        lax.dot_general(
            activated, all_cots, (((0,), (0,)), ((), ())), preferred_element_type=F32
        )
        * norm_factor
    )
    return (grad_tokens.astype(BF16), grad_up.astype(BF16), grad_down.astype(BF16))


def solution(mesh):
    fine = Mesh(mesh.devices.reshape(4, 2, 2, 8, 2), ROW + COL)
    placed = (P(COL, ROW), P(ROW, COL), P(COL), P(COL, ROW), P(COL, ROW))
    return jax.shard_map(
        on_device,
        mesh=fine,
        in_specs=placed,
        out_specs=(P(COL, ROW), P(ROW, COL), P(COL, ROW)),
        check_vma=False,
    )
```

```python
import functools
import math

import jax
import jax.numpy as jnp
from jax import lax
from jax.experimental import pallas as pl
from jax.experimental.pallas import tpu as pltpu
from jax.sharding import Mesh, PartitionSpec as P

ROW = ("y", "x_hi")
COL = ("x_lo", "z", "core")
BF16 = jnp.bfloat16
F32 = jnp.float32
ZN = 8
RN = 8
EARLY = (0, -1, 1, -2, 2)
LATE = (-3, 3, 4)
BLOCKS = tuple((side, k) for group in (EARLY, LATE) for side in (0, 1) for k in group)
WHOLE = pl.BlockSpec(memory_space=pltpu.VMEM)


def light():
    return pl.CostEstimate(flops=1, bytes_accessed=1, transcendentals=0)


def params(steps):
    return pltpu.CompilerParams(
        dimension_semantics=("arbitrary",) * steps, vmem_limit_bytes=24 * 2**20
    )


def gelu_value(hidden):
    return hidden * 0.5 * (1.0 + lax.erf(hidden / math.sqrt(2.0)))


def gelu_slope(hidden):
    cumulative = 0.5 * (1.0 + lax.erf(hidden / math.sqrt(2.0)))
    density = jnp.exp(-0.5 * hidden * hidden) / math.sqrt(2.0 * math.pi)
    return cumulative + hidden * density


def shift_z(x, k):
    return lax.ppermute(x, "z", [(i, (i + k) % ZN) for i in range(ZN)])


def swap(x, axis):
    return lax.ppermute(x, axis, [(0, 1), (1, 0)])


def dot(a, b):
    return jnp.dot(a, b, preferred_element_type=F32)


def dot_t(a, b):
    return lax.dot_general(a, b, (((1,), (1,)), ((), ())), preferred_element_type=F32)


def dot_rows(a, b):
    return lax.dot_general(a, b, (((0,), (0,)), ((), ())), preferred_element_type=F32)


def project_kernel(pieces, width, units, tile, *refs):
    given, (up, down, out, rows) = refs[:pieces], refs[pieces:]

    @pl.when(pl.program_id(0) == 0)
    def _():
        base = 0
        for piece in given:
            rows[base : base + piece.shape[0], :] = piece[...]
            base += piece.shape[0]

    at = pl.multiple_of(pl.program_id(0) * tile, tile)
    later = pl.multiple_of(units + pl.program_id(0) * tile, tile)
    out[:, pl.ds(at, tile)] = dot(rows[:, :width], up[...]).astype(BF16)
    out[:, pl.ds(later, tile)] = dot_t(rows[:, width:], down[...]).astype(BF16)


def project(pieces, up, down):
    width, units = up.shape
    tile = units // 3
    count = sum(piece.shape[0] for piece in pieces)
    return pl.pallas_call(
        functools.partial(project_kernel, len(pieces), width, units, tile),
        grid=(3,),
        out_shape=jax.ShapeDtypeStruct((count, 2 * units), BF16),
        in_specs=[pl.BlockSpec(piece.shape, lambda j: (0, 0)) for piece in pieces]
        + [
            pl.BlockSpec((width, tile), lambda j: (0, j)),
            pl.BlockSpec((tile, width), lambda j: (j, 0)),
        ],
        out_specs=pl.BlockSpec((count, 2 * units), lambda j: (0, 0)),
        scratch_shapes=[pltpu.VMEM((count, 2 * width), BF16)],
        compiler_params=params(1),
        cost_estimate=light(),
        name="project",
    )(*pieces, up, down)


def pointwise_kernel(units, parts, bias, out):
    count = parts.shape[0] // RN
    sums = parts[:count, :].astype(F32)
    for r in range(1, RN):
        sums += parts[r * count : (r + 1) * count, :].astype(F32)
    hidden = sums[:, :units] + bias[...].astype(F32)
    activated = gelu_value(hidden).astype(BF16)
    hidden_grad = (sums[:, units:] * gelu_slope(hidden)).astype(BF16)
    for r in range(RN):
        out[r * count : (r + 1) * count, :units] = activated
        out[r * count : (r + 1) * count, units:] = hidden_grad


def pointwise(parts, bias):
    units = bias.shape[0]
    return pl.pallas_call(
        functools.partial(pointwise_kernel, units),
        out_shape=jax.ShapeDtypeStruct(parts.shape, BF16),
        in_specs=[WHOLE] * 2,
        out_specs=WHOLE,
        compiler_params=params(0),
        cost_estimate=light(),
        name="pointwise",
    )(parts, bias.reshape(1, units))


def place(where, grads, rows, share, core):
    z, x = where[0], where[1]
    for i, (side, k) in enumerate(BLOCKS):
        owner = lax.rem(z + k + ZN, ZN) + ZN * (1 - x if side else x)
        at = pl.multiple_of(owner * share, share)
        base = (core * len(BLOCKS) + i) * share
        rows[pl.ds(at, share), :] = grads[base : base + share, :]


def others_kernel(share, where, grads, up, out, rows):
    @pl.when(pl.program_id(0) == 0)
    def _():
        place(where, grads, rows, share, 1)

    out[...] = dot_t(rows[...], up[...]).astype(BF16)


def mine_kernel(share, where, grads, up, given, out, rows):
    @pl.when(pl.program_id(0) == 0)
    def _():
        place(where, grads, rows, share, 0)

    out[...] = (dot_t(rows[...], up[...]) + given[...].astype(F32)).astype(BF16)


def back(where, both, up, given, share):
    width, units = up.shape
    count = both.shape[0] // 2
    tile = width // 3
    block = pl.BlockSpec((count, tile), lambda j: (0, j))
    more = [] if given is None else [given]
    return pl.pallas_call(
        functools.partial(others_kernel if given is None else mine_kernel, share),
        grid=(3,),
        out_shape=jax.ShapeDtypeStruct((count, width), BF16),
        in_specs=[
            pl.BlockSpec(memory_space=pltpu.SMEM),
            pl.BlockSpec((2 * count, units), lambda j: (0, 1)),
            pl.BlockSpec((tile, units), lambda j: (j, 0)),
        ]
        + [block] * len(more),
        out_specs=block,
        scratch_shapes=[pltpu.VMEM((count, units), BF16)],
        compiler_params=params(1),
        cost_estimate=light(),
        name="back",
    )(where, both, up, *more)


def collect_kernel(parts, out):
    count = out.shape[0]
    sums = parts[:count, :].astype(F32)
    for r in range(1, parts.shape[0] // count):
        sums += parts[r * count : (r + 1) * count, :].astype(F32)
    out[...] = sums.astype(BF16)


def collect(parts, share):
    return pl.pallas_call(
        collect_kernel,
        out_shape=jax.ShapeDtypeStruct((share, parts.shape[1]), BF16),
        in_specs=[WHOLE],
        out_specs=WHOLE,
        compiler_params=params(0),
        cost_estimate=light(),
        name="collect",
    )(parts)


def on_device(tokens, up_weight, up_bias, down_weight, cotangent):
    width, units = up_weight.shape
    share = tokens.shape[0]
    where = jnp.stack([lax.axis_index("z"), lax.axis_index("x_lo")]).astype(jnp.int32)

    held = {0: jnp.concatenate([tokens, cotangent], axis=1)}
    across = {0: swap(held[0], "x_lo")}
    for k in range(1, ZN // 2):
        held[-k] = shift_z(held[1 - k], 1)
        held[k] = shift_z(held[k - 1], -1)
        pair = swap(jnp.concatenate([held[-k], held[k]], axis=0), "x_lo")
        across[-k], across[k] = pair[:share], pair[share:]
    held[ZN // 2] = shift_z(held[ZN // 2 - 1], -1)
    across[ZN // 2] = swap(held[ZN // 2], "x_lo")

    mine = [
        jnp.concatenate([held[k] for k in group] + [across[k] for k in group], axis=0)
        for group in (EARLY, LATE)
    ]
    pieces = mine + [swap(piece, "core") for piece in mine]

    parts = project(pieces, up_weight, down_weight)
    parts = lax.all_to_all(parts, ROW, 0, 0, tiled=True)
    both = pointwise(parts, up_bias)
    both = lax.all_to_all(both, ROW, 0, 0, tiled=True)

    other = swap(back(where, both, up_weight, None, share), "core")
    near = back(where, both, up_weight, other, share)
    near = lax.all_to_all(near, ("x_lo", "z"), 0, 0, tiled=True)
    grad_tokens = collect(near, share)

    all_rows = jnp.concatenate(pieces, axis=0)
    norm_factor = 1.0 / math.sqrt(all_rows.shape[0])
    grad_up = dot_rows(all_rows[:, :width], both[:, units:]) * norm_factor
    grad_down = dot_rows(both[:, :units], all_rows[:, width:]) * norm_factor
    return (grad_tokens, grad_up.astype(BF16), grad_down.astype(BF16))


def solution(mesh):
    fine = Mesh(mesh.devices.reshape(4, 2, 2, 8, 2), ROW + COL)
    placed = (P(COL, ROW), P(ROW, COL), P(COL), P(COL, ROW), P(COL, ROW))
    return jax.shard_map(
        on_device,
        mesh=fine,
        in_specs=placed,
        out_specs=(P(COL, ROW), P(ROW, COL), P(COL, ROW)),
        check_vma=False,
    )
```

```python
import functools
import math

import jax
import jax.numpy as jnp
from jax import lax
from jax.experimental import pallas as pl
from jax.experimental.pallas import tpu as pltpu
from jax.sharding import Mesh, PartitionSpec as P

ROW = ("y", "x_hi")
COL = ("x_lo", "z", "core")
BF16 = jnp.bfloat16
F32 = jnp.float32
ZN = 8
RN = 8
BLOCKS = tuple((side, k) for k in (0, -1, -2, -3, 1, 2, 3, 4) for side in (0, 1))
WHOLE = pl.BlockSpec(memory_space=pltpu.VMEM)
UNREAD = pl.BlockSpec(memory_space=pl.ANY)


def light():
    return pl.CostEstimate(flops=1, bytes_accessed=1, transcendentals=0)


def params(steps):
    return pltpu.CompilerParams(
        dimension_semantics=("arbitrary",) * steps, vmem_limit_bytes=56 * 2**20
    )


def gelu_value(hidden):
    return hidden * 0.5 * (1.0 + lax.erf(hidden / math.sqrt(2.0)))


def gelu_slope(hidden):
    cumulative = 0.5 * (1.0 + lax.erf(hidden / math.sqrt(2.0)))
    density = jnp.exp(-0.5 * hidden * hidden) / math.sqrt(2.0 * math.pi)
    return cumulative + hidden * density


def shift_z(x, k):
    return lax.ppermute(x, "z", [(i, (i + k) % ZN) for i in range(ZN)])


def swap(x, axis):
    return lax.ppermute(x, axis, [(0, 1), (1, 0)])


def dot(a, b):
    return jnp.dot(a, b, preferred_element_type=F32)


def dot_t(a, b):
    return lax.dot_general(a, b, (((1,), (1,)), ((), ())), preferred_element_type=F32)


def dot_rows(a, b):
    return lax.dot_general(a, b, (((0,), (0,)), ((), ())), preferred_element_type=F32)


def pack_kernel(tokens, cotangent, out):
    width = tokens.shape[1]
    out[:, :width] = tokens[...]
    out[:, width:] = cotangent[...]


def pack(tokens, cotangent):
    return pl.pallas_call(
        pack_kernel,
        out_shape=jax.ShapeDtypeStruct((tokens.shape[0], 2 * tokens.shape[1]), BF16),
        in_specs=[WHOLE] * 2,
        out_specs=WHOLE,
        compiler_params=params(0),
        cost_estimate=light(),
        name="pack",
    )(tokens, cotangent)


def project_kernel(pieces, width, *refs):
    given, (up, up_two, down, down_two, out, kept, rows, sem) = refs[:pieces], refs[pieces:]
    j = pl.program_id(0)
    keep = pltpu.make_async_copy(rows, kept, sem)

    @pl.when(j == 0)
    def _():
        base = 0
        for piece in given:
            rows[base : base + piece.shape[0], :] = piece[...]
            base += piece.shape[0]
        keep.start()

    for step, weight in ((0, up), (1, up_two)):

        @pl.when(j // 2 == step)
        def _():
            out[...] = dot(rows[:, :width], weight[...]).astype(BF16)

    for step, weight in ((2, down), (3, down_two)):

        @pl.when(j // 2 == step)
        def _():
            out[...] = dot_t(rows[:, width:], weight[...]).astype(BF16)

    @pl.when(j == 7)
    def _():
        keep.wait()


def project(pieces, up, up_two, down, down_two):
    width, units = up.shape
    tile = units // 2
    count = sum(piece.shape[0] for piece in pieces)

    def columns(first):
        return pl.BlockSpec((width, tile), lambda j: (0, jnp.clip(j - first, 0, 1)))

    def lines(first):
        return pl.BlockSpec((tile, width), lambda j: (jnp.clip(j - first, 0, 1), 0))

    return pl.pallas_call(
        functools.partial(project_kernel, len(pieces), width),
        grid=(8,),
        out_shape=[
            jax.ShapeDtypeStruct((count, 4 * units), BF16),
            jax.ShapeDtypeStruct((count, 2 * width), BF16),
        ],
        in_specs=[pl.BlockSpec(piece.shape, lambda j: (0, 0)) for piece in pieces]
        + [columns(0), columns(2), lines(4), lines(6)],
        out_specs=[pl.BlockSpec((count, tile), lambda j: (0, j)), UNREAD],
        scratch_shapes=[pltpu.VMEM((count, 2 * width), BF16), pltpu.SemaphoreType.DMA],
        compiler_params=params(1),
        cost_estimate=light(),
        name="project",
    )(*pieces, up, up_two, down, down_two)


def pointwise_kernel(parts, bias, bias_two, out):
    count = parts.shape[0] // RN
    units = parts.shape[1] // 4
    for k, offset in enumerate((bias, bias_two)):
        hidden = offset[...].astype(F32) + jnp.zeros((count, units), F32)
        act_grad = jnp.zeros((count, units), F32)
        for r in range(RN):
            some = parts[r * count : (r + 1) * count, :]
            hidden += some[:, k * units : (k + 1) * units].astype(F32)
            act_grad += some[:, (2 + k) * units : (3 + k) * units].astype(F32)
        activated = gelu_value(hidden).astype(BF16)
        hidden_grad = (act_grad * gelu_slope(hidden)).astype(BF16)
        at = (3 - k) * units
        for r in range(RN):
            out[r * count : (r + 1) * count, k * units : (k + 1) * units] = hidden_grad
            out[r * count : (r + 1) * count, at : at + units] = activated


def pointwise(parts, bias, bias_two):
    return pl.pallas_call(
        pointwise_kernel,
        out_shape=jax.ShapeDtypeStruct(parts.shape, BF16),
        in_specs=[WHOLE] * 3,
        out_specs=WHOLE,
        compiler_params=params(0),
        cost_estimate=light(),
        name="pointwise",
    )(parts, bias.reshape(1, -1), bias_two.reshape(1, -1))


def back_kernel(share, where, grads, up, up_two, out, rows):
    units = up.shape[1]

    @pl.when(pl.program_id(0) == 0)
    def _():
        z, x = where[0], where[1]
        for i, (side, k) in enumerate(BLOCKS):
            owner = lax.rem(z + k + ZN, ZN) + ZN * (1 - x if side else x)
            at = pl.multiple_of(owner * share, share)
            rows[pl.ds(at, share), :] = grads[i * share : (i + 1) * share, :]

    part = dot_t(rows[:, :units], up[...]) + dot_t(rows[:, units:], up_two[...])
    out[...] = part.astype(BF16)


def back(where, both, up, up_two, share):
    width, units = up.shape
    count = both.shape[0]
    tile = width // 3
    return pl.pallas_call(
        functools.partial(back_kernel, share),
        grid=(3,),
        out_shape=jax.ShapeDtypeStruct((count, width), BF16),
        in_specs=[
            pl.BlockSpec(memory_space=pltpu.SMEM),
            pl.BlockSpec((count, 2 * units), lambda j: (0, 0)),
            pl.BlockSpec((tile, units), lambda j: (j, 0)),
            pl.BlockSpec((tile, units), lambda j: (j, 0)),
        ],
        out_specs=pl.BlockSpec((count, tile), lambda j: (0, j)),
        scratch_shapes=[pltpu.VMEM((count, 2 * units), BF16)],
        compiler_params=params(1),
        cost_estimate=light(),
        name="back",
    )(where, both, up, up_two)


def collect_kernel(parts, out):
    count = out.shape[0]
    sums = parts[:count, :].astype(F32)
    for r in range(1, parts.shape[0] // count):
        sums += parts[r * count : (r + 1) * count, :].astype(F32)
    out[...] = sums.astype(BF16)


def collect(parts, share):
    return pl.pallas_call(
        collect_kernel,
        out_shape=jax.ShapeDtypeStruct((share, parts.shape[1]), BF16),
        in_specs=[WHOLE],
        out_specs=WHOLE,
        compiler_params=params(0),
        cost_estimate=light(),
        name="collect",
    )(parts)


def outer_kernel(factor, left, left_two, right, right_two, out):
    sums = dot_rows(left[...], right[...]) + dot_rows(left_two[...], right_two[...])
    out[...] = (sums * factor).astype(BF16)


def outer(factor, tiles, left, left_two, right, right_two):
    count = left[0].shape[0]
    size = left[2] // tiles

    def tiled(given):
        array, first, columns = given
        return pl.BlockSpec((count, size), lambda j: (0, first * tiles + j))

    def full(given):
        array, first, columns = given
        return pl.BlockSpec((count, columns), lambda j: (0, first))

    return pl.pallas_call(
        functools.partial(outer_kernel, factor),
        grid=(tiles,),
        out_shape=jax.ShapeDtypeStruct((left[2], right[2]), BF16),
        in_specs=[tiled(left), tiled(left_two), full(right), full(right_two)],
        out_specs=pl.BlockSpec((size, right[2]), lambda j: (j, 0)),
        compiler_params=params(1),
        cost_estimate=light(),
        name="outer",
    )(left[0], left_two[0], right[0], right_two[0])


def on_device(tokens, up_weight, up_bias, down_weight, cotangent):
    width, units = up_weight.shape
    share = tokens.shape[0]
    where = jnp.stack([lax.axis_index("z"), lax.axis_index("x_lo")]).astype(jnp.int32)

    held = pack(tokens, cotangent)
    across = swap(held, "x_lo")
    pieces = [held, across]
    forward = jnp.concatenate([held, across], axis=0)
    backward = held
    fore, aft = [], []
    for k in range(1, ZN // 2 + 1):
        backward = shift_z(backward, -1)
        if k < ZN // 2:
            forward = shift_z(forward, 1)
            fore.append(forward)
        aft += [backward, swap(backward, "x_lo")]
    pieces += fore + aft

    up_two, down_two, bias_two = (swap(w, "core") for w in (up_weight, down_weight, up_bias))
    parts, rows = project(pieces, up_weight, up_two, down_weight, down_two)
    parts = lax.all_to_all(parts, ROW, 0, 0, tiled=True)
    both = pointwise(parts, up_bias, bias_two)
    both = lax.all_to_all(both, ROW, 0, 0, tiled=True)

    near = back(where, both, up_weight, up_two, share)
    near = lax.all_to_all(near, ("x_lo", "z"), 0, 0, tiled=True)
    grad_tokens = collect(near, share)

    rows_two = swap(rows, "core")
    both_two = swap(both[:, units : 3 * units], "core")
    factor = 1.0 / math.sqrt(2 * rows.shape[0])
    grad_up = outer(
        factor, 3, (rows, 0, width), (rows_two, 0, width), (both, 0, units), (both_two, 0, units)
    )
    grad_down = outer(
        factor, 3, (both, 3, units), (both_two, 1, units), (rows, 1, width), (rows_two, 1, width)
    )
    return (grad_tokens, grad_up, grad_down)


def solution(mesh):
    fine = Mesh(mesh.devices.reshape(4, 2, 2, 8, 2), ROW + COL)
    placed = (P(COL, ROW), P(ROW, COL), P(COL), P(COL, ROW), P(COL, ROW))
    return jax.shard_map(
        on_device,
        mesh=fine,
        in_specs=placed,
        out_specs=(P(COL, ROW), P(ROW, COL), P(COL, ROW)),
        check_vma=False,
    )
```

```python
import functools
import math

import jax
import jax.numpy as jnp
from jax import lax
from jax.experimental import pallas as pl
from jax.experimental.pallas import tpu as pltpu
from jax.sharding import Mesh, PartitionSpec as P

ROW = ("y", "x_hi")
COL = ("x_lo", "z", "core")
BF16 = jnp.bfloat16
F32 = jnp.float32
ZN = 8
RN = 8
BLOCKS = tuple((side, k) for k in (0, -1, -2, -3, 1, 2, 3, 4) for side in (0, 1))
WHOLE = pl.BlockSpec(memory_space=pltpu.VMEM)
REMAIN = pl.BlockSpec(memory_space=pl.ANY)
FAR = pl.BlockSpec(memory_space=pltpu.HBM)


def light():
    return pl.CostEstimate(flops=1, bytes_accessed=1, transcendentals=0)


def heavy():
    return pl.CostEstimate(flops=2 * 10**10, bytes_accessed=2 * 10**6, transcendentals=0)


def params(steps):
    return pltpu.CompilerParams(
        dimension_semantics=("arbitrary",) * steps, vmem_limit_bytes=20 * 2**20
    )


def gelu_value(hidden):
    return hidden * 0.5 * (1.0 + lax.erf(hidden / math.sqrt(2.0)))


def gelu_slope(hidden):
    cumulative = 0.5 * (1.0 + lax.erf(hidden / math.sqrt(2.0)))
    density = jnp.exp(-0.5 * hidden * hidden) / math.sqrt(2.0 * math.pi)
    return cumulative + hidden * density


def shift_z(x, k):
    return lax.ppermute(x, "z", [(i, (i + k) % ZN) for i in range(ZN)])


def swap(x, axis):
    return lax.ppermute(x, axis, [(0, 1), (1, 0)])


def dot(a, b):
    return jnp.dot(a, b, preferred_element_type=F32)


def dot_t(a, b):
    return lax.dot_general(a, b, (((1,), (1,)), ((), ())), preferred_element_type=F32)


def dot_rows(a, b):
    return lax.dot_general(a, b, (((0,), (0,)), ((), ())), preferred_element_type=F32)


def pack_kernel(tokens, cotangent, out):
    width = tokens.shape[1]
    out[:, :width] = tokens[...]
    out[:, width:] = cotangent[...]


def pack(tokens, cotangent):
    return pl.pallas_call(
        pack_kernel,
        out_shape=jax.ShapeDtypeStruct((tokens.shape[0], 2 * tokens.shape[1]), BF16),
        in_specs=[WHOLE] * 2,
        out_specs=WHOLE,
        compiler_params=params(0),
        cost_estimate=heavy(),
        name="pack",
    )(tokens, cotangent)


def project_kernel(pieces, width, units, *refs):
    given, weights = refs[:pieces], refs[pieces : pieces + 4]
    out, kept, rows, made, sems = refs[pieces + 4 :]
    loads, base = [], 0
    for piece in given:
        at = rows.at[base : base + piece.shape[0], :]
        loads.append(pltpu.make_async_copy(piece, at, sems.at[len(loads)]))
        base += piece.shape[0]
    for copy in loads:
        copy.start()
    for copy in loads:
        copy.wait()
    sends = [pltpu.make_async_copy(rows, kept, sems.at[pieces])]
    sends[0].start()
    for k, weight in enumerate(weights):
        at = slice(k * units, (k + 1) * units)
        if k < 2:
            product = dot(rows[:, :width], weight[...])
        else:
            product = dot_t(rows[:, width:], weight[...])
        made[:, at] = product.astype(BF16)
        sends.append(
            pltpu.make_async_copy(made.at[:, at], out.at[:, at], sems.at[pieces + 1 + k])
        )
        sends[-1].start()
    for copy in sends:
        copy.wait()


def project(pieces, up, up_two, down, down_two):
    width, units = up.shape
    count = sum(piece.shape[0] for piece in pieces)
    return pl.pallas_call(
        functools.partial(project_kernel, len(pieces), width, units),
        out_shape=[
            pltpu.HBM((count, 4 * units), BF16),
            jax.ShapeDtypeStruct((count, 2 * width), BF16),
        ],
        in_specs=[REMAIN] * len(pieces) + [WHOLE] * 4,
        out_specs=[FAR, REMAIN],
        scratch_shapes=[
            pltpu.VMEM((count, 2 * width), BF16),
            pltpu.VMEM((count, 4 * units), BF16),
            pltpu.SemaphoreType.DMA((len(pieces) + 5,)),
        ],
        compiler_params=params(0),
        cost_estimate=light(),
        name="project",
    )(*pieces, up, up_two, down, down_two)


def pointwise_kernel(parts, bias, bias_two, out, made, sems):
    count = parts.shape[0] // RN
    units = parts.shape[1] // 4
    for k, offset in enumerate((bias, bias_two)):
        hidden = offset[...].astype(F32) + jnp.zeros((count, units), F32)
        act_grad = jnp.zeros((count, units), F32)
        for r in range(RN):
            some = parts[r * count : (r + 1) * count, :]
            hidden += some[:, k * units : (k + 1) * units].astype(F32)
            act_grad += some[:, (2 + k) * units : (3 + k) * units].astype(F32)
        activated = gelu_value(hidden).astype(BF16)
        hidden_grad = (act_grad * gelu_slope(hidden)).astype(BF16)
        at = (3 - k) * units
        made[:, k * units : (k + 1) * units] = hidden_grad
        made[:, at : at + units] = activated
    sends = [
        pltpu.make_async_copy(made, out.at[r * count : (r + 1) * count, :], sems.at[r])
        for r in range(RN)
    ]
    for send in sends:
        send.start()
    for send in sends:
        send.wait()


def pointwise(parts, bias, bias_two):
    return pl.pallas_call(
        pointwise_kernel,
        out_shape=pltpu.HBM(parts.shape, BF16),
        in_specs=[WHOLE] * 3,
        out_specs=FAR,
        scratch_shapes=[
            pltpu.VMEM((parts.shape[0] // RN, parts.shape[1]), BF16),
            pltpu.SemaphoreType.DMA((RN,)),
        ],
        compiler_params=params(0),
        cost_estimate=heavy(),
        name="pointwise",
    )(parts, bias.reshape(1, -1), bias_two.reshape(1, -1))


def back_kernel(share, where, grads, up, up_two, out, rows, made, sems):
    width, units = up.shape
    tile = width // 3
    z, x = where[0], where[1]
    loads, sends = [], []
    for i, (side, k) in enumerate(BLOCKS):
        owner = lax.rem(z + k + ZN, ZN) + ZN * (1 - x if side else x)
        at = pl.multiple_of(owner * share, share)
        source = grads.at[i * share : (i + 1) * share, : 2 * units]
        loads.append(pltpu.make_async_copy(source, rows.at[pl.ds(at, share), :], sems.at[i]))
    for copy in loads:
        copy.start()
    for copy in loads:
        copy.wait()
    for t in range(3):
        part = slice(t * tile, (t + 1) * tile)
        product = dot_t(rows[:, :units], up[part, :]) + dot_t(rows[:, units:], up_two[part, :])
        made[:, part] = product.astype(BF16)
        sends.append(
            pltpu.make_async_copy(made.at[:, part], out.at[:, part], sems.at[len(BLOCKS) + t])
        )
        sends[-1].start()
    for copy in sends:
        copy.wait()


def back(where, both, up, up_two, share):
    width, units = up.shape
    count = both.shape[0]
    return pl.pallas_call(
        functools.partial(back_kernel, share),
        out_shape=pltpu.HBM((count, width), BF16),
        in_specs=[pl.BlockSpec(memory_space=pltpu.SMEM), REMAIN, WHOLE, WHOLE],
        out_specs=FAR,
        scratch_shapes=[
            pltpu.VMEM((count, 2 * units), BF16),
            pltpu.VMEM((count, width), BF16),
            pltpu.SemaphoreType.DMA((len(BLOCKS) + 3,)),
        ],
        compiler_params=params(0),
        cost_estimate=light(),
        name="back",
    )(where, both, up, up_two)


def collect_kernel(parts, out, held, sems):
    count = out.shape[0]
    loads = []
    for r in range(4):
        at = slice(r * held.shape[0] // 4, (r + 1) * held.shape[0] // 4)
        loads.append(pltpu.make_async_copy(parts.at[at, :], held.at[at, :], sems.at[r]))
    for copy in loads:
        copy.start()
    sums = jnp.zeros(out.shape, F32)
    for r in range(held.shape[0] // count):
        if r * count % (held.shape[0] // 4) == 0:
            loads[r * count // (held.shape[0] // 4)].wait()
        sums += held[r * count : (r + 1) * count, :].astype(F32)
    out[...] = sums.astype(BF16)


def collect(parts, share):
    return pl.pallas_call(
        collect_kernel,
        out_shape=jax.ShapeDtypeStruct((share, parts.shape[1]), BF16),
        in_specs=[REMAIN],
        out_specs=WHOLE,
        scratch_shapes=[pltpu.VMEM(parts.shape, BF16), pltpu.SemaphoreType.DMA((4,))],
        compiler_params=params(0),
        cost_estimate=light(),
        name="collect",
    )(parts)


def outer_kernel(factor, left, left_two, right, right_two, out):
    sums = dot_rows(left[...], right[...]) + dot_rows(left_two[...], right_two[...])
    out[...] = (sums * factor).astype(BF16)


def outer(factor, tiles, left, left_two, right, right_two):
    count = left[0].shape[0]
    size = left[2] // tiles

    def tiled(given):
        array, first, columns = given
        return pl.BlockSpec((count, size), lambda j: (0, first * tiles + j))

    def full(given):
        array, first, columns = given
        return pl.BlockSpec((count, columns), lambda j: (0, first))

    return pl.pallas_call(
        functools.partial(outer_kernel, factor),
        grid=(tiles,),
        out_shape=jax.ShapeDtypeStruct((left[2], right[2]), BF16),
        in_specs=[tiled(left), tiled(left_two), full(right), full(right_two)],
        out_specs=pl.BlockSpec((size, right[2]), lambda j: (j, 0)),
        compiler_params=params(1),
        cost_estimate=light(),
        name="outer",
    )(left[0], left_two[0], right[0], right_two[0])


def on_device(tokens, up_weight, up_bias, down_weight, cotangent):
    width, units = up_weight.shape
    share = tokens.shape[0]
    where = jnp.stack([lax.axis_index("z"), lax.axis_index("x_lo")]).astype(jnp.int32)

    held = pack(tokens, cotangent)
    across = swap(held, "x_lo")
    pieces = [held, across]
    forward = jnp.concatenate([held, across], axis=0)
    backward = held
    fore, aft = [], []
    for k in range(1, ZN // 2 + 1):
        backward = shift_z(backward, -1)
        if k < ZN // 2:
            forward = shift_z(forward, 1)
            fore.append(forward)
        aft += [backward, swap(backward, "x_lo")]
    pieces += fore + aft

    up_two, down_two, bias_two = (swap(w, "core") for w in (up_weight, down_weight, up_bias))
    parts, rows = project(pieces, up_weight, up_two, down_weight, down_two)
    parts = lax.all_to_all(parts, ROW, 0, 0, tiled=True)
    both = pointwise(parts, up_bias, bias_two)
    both = lax.all_to_all(both, ROW, 0, 0, tiled=True)

    near = back(where, both, up_weight, up_two, share)
    near = lax.all_to_all(near, ("x_lo", "z"), 0, 0, tiled=True)
    grad_tokens = collect(near, share)

    rows_two = swap(rows, "core")
    both_two = swap(both[:, units : 3 * units], "core")
    factor = 1.0 / math.sqrt(2 * rows.shape[0])
    grad_up = outer(
        factor, 3, (rows, 0, width), (rows_two, 0, width), (both, 0, units), (both_two, 0, units)
    )
    grad_down = outer(
        factor, 3, (both, 3, units), (both_two, 1, units), (rows, 1, width), (rows_two, 1, width)
    )
    return (grad_tokens, grad_up, grad_down)


def solution(mesh):
    fine = Mesh(mesh.devices.reshape(4, 2, 2, 8, 2), ROW + COL)
    placed = (P(COL, ROW), P(ROW, COL), P(COL), P(COL, ROW), P(COL, ROW))
    return jax.shard_map(
        on_device,
        mesh=fine,
        in_specs=placed,
        out_specs=(P(COL, ROW), P(ROW, COL), P(COL, ROW)),
        check_vma=False,
    )
```

```python
import functools
import math

import jax
import jax.numpy as jnp
from jax import lax
from jax.experimental import pallas as pl
from jax.experimental.pallas import tpu as pltpu
from jax.sharding import Mesh, PartitionSpec as P

ROW = ("y", "x_hi")
COL = ("x_lo", "z", "core")
BF16 = jnp.bfloat16
F32 = jnp.float32
ZN = 8
RN = 8
BLOCKS = tuple((side, k) for k in (0, -1, -2, -3, 1, 2, 3, 4) for side in (0, 1))
WHOLE = pl.BlockSpec(memory_space=pltpu.VMEM)
REMAIN = pl.BlockSpec(memory_space=pl.ANY)
FAR = pl.BlockSpec(memory_space=pltpu.HBM)


def in_hbm(x):
    return pltpu.with_memory_space_constraint(x, pltpu.HBM)


def in_vmem(x):
    return pltpu.with_memory_space_constraint(x, pltpu.VMEM)


def light():
    return pl.CostEstimate(flops=1, bytes_accessed=1, transcendentals=0)


def heavy():
    return pl.CostEstimate(flops=2 * 10**10, bytes_accessed=2 * 10**6, transcendentals=0)


def params(steps):
    return pltpu.CompilerParams(
        dimension_semantics=("arbitrary",) * steps, vmem_limit_bytes=20 * 2**20
    )


def gelu_value(hidden):
    return hidden * 0.5 * (1.0 + lax.erf(hidden / math.sqrt(2.0)))


def gelu_slope(hidden):
    cumulative = 0.5 * (1.0 + lax.erf(hidden / math.sqrt(2.0)))
    density = jnp.exp(-0.5 * hidden * hidden) / math.sqrt(2.0 * math.pi)
    return cumulative + hidden * density


def shift_z(x, k):
    return lax.ppermute(x, "z", [(i, (i + k) % ZN) for i in range(ZN)])


def swap(x, axis):
    return lax.ppermute(x, axis, [(0, 1), (1, 0)])


def dot(a, b):
    return jnp.dot(a, b, preferred_element_type=F32)


def dot_t(a, b):
    return lax.dot_general(a, b, (((1,), (1,)), ((), ())), preferred_element_type=F32)


def dot_rows(a, b):
    return lax.dot_general(a, b, (((0,), (0,)), ((), ())), preferred_element_type=F32)


def pack_kernel(tokens, cotangent, out, sems):
    width = tokens.shape[1]
    copies = [
        pltpu.make_async_copy(tokens, out.at[:, :width], sems.at[0]),
        pltpu.make_async_copy(cotangent, out.at[:, width:], sems.at[1]),
    ]
    for copy in copies:
        copy.start()
    for copy in copies:
        copy.wait()


def pack(tokens, cotangent):
    return pl.pallas_call(
        pack_kernel,
        out_shape=jax.ShapeDtypeStruct((tokens.shape[0], 2 * tokens.shape[1]), BF16),
        in_specs=[FAR] * 2,
        out_specs=REMAIN,
        scratch_shapes=[pltpu.SemaphoreType.DMA((2,))],
        compiler_params=params(0),
        cost_estimate=heavy(),
        name="pack",
    )(in_hbm(tokens), in_hbm(cotangent))


def project_kernel(pieces, width, units, *refs):
    given, weights = refs[:pieces], refs[pieces : pieces + 4]
    out, kept, rows, made, sems = refs[pieces + 4 :]
    loads, base = [], 0
    for piece in given:
        at = rows.at[base : base + piece.shape[0], :]
        loads.append(pltpu.make_async_copy(piece, at, sems.at[len(loads)]))
        base += piece.shape[0]
    for copy in loads:
        copy.start()
    for copy in loads:
        copy.wait()
    sends = [
        pltpu.make_async_copy(rows, kept, sems.at[pieces]),
    ]
    for copy in sends:
        copy.start()
    for k, weight in enumerate(weights):
        at = slice(k * units, (k + 1) * units)
        if k < 2:
            product = dot(rows[:, :width], weight[...])
        else:
            product = dot_t(rows[:, width:], weight[...])
        made[:, at] = product.astype(BF16)
        sends.append(
            pltpu.make_async_copy(made.at[:, at], out.at[:, at], sems.at[pieces + 1 + k])
        )
        sends[-1].start()
    for copy in sends:
        copy.wait()


def project(pieces, up, up_two, down, down_two):
    width, units = up.shape
    count = sum(piece.shape[0] for piece in pieces)
    return pl.pallas_call(
        functools.partial(project_kernel, len(pieces), width, units),
        out_shape=[
            pltpu.HBM((count, 4 * units), BF16),
            jax.ShapeDtypeStruct((count, 2 * width), BF16),
        ],
        in_specs=[REMAIN] * len(pieces) + [WHOLE] * 4,
        out_specs=[FAR, REMAIN],
        scratch_shapes=[
            pltpu.VMEM((count, 2 * width), BF16),
            pltpu.VMEM((count, 4 * units), BF16),
            pltpu.SemaphoreType.DMA((len(pieces) + 5,)),
        ],
        compiler_params=params(0),
        cost_estimate=light(),
        name="project",
    )(*pieces, up, up_two, down, down_two)


def pointwise_kernel(parts, bias, bias_two, out, made, sems):
    count = parts.shape[0] // RN
    units = parts.shape[1] // 4
    for k, offset in enumerate((bias, bias_two)):
        hidden = offset[...].astype(F32) + jnp.zeros((count, units), F32)
        act_grad = jnp.zeros((count, units), F32)
        for r in range(RN):
            some = parts[r * count : (r + 1) * count, :]
            hidden += some[:, k * units : (k + 1) * units].astype(F32)
            act_grad += some[:, (2 + k) * units : (3 + k) * units].astype(F32)
        activated = gelu_value(hidden).astype(BF16)
        hidden_grad = (act_grad * gelu_slope(hidden)).astype(BF16)
        at = (3 - k) * units
        made[:, k * units : (k + 1) * units] = hidden_grad
        made[:, at : at + units] = activated
    sends = [
        pltpu.make_async_copy(made, out.at[r * count : (r + 1) * count, :], sems.at[r])
        for r in range(RN)
    ]
    for send in sends:
        send.start()
    for send in sends:
        send.wait()


def pointwise(parts, bias, bias_two):
    return pl.pallas_call(
        pointwise_kernel,
        out_shape=pltpu.HBM(parts.shape, BF16),
        in_specs=[WHOLE] * 3,
        out_specs=FAR,
        scratch_shapes=[
            pltpu.VMEM((parts.shape[0] // RN, parts.shape[1]), BF16),
            pltpu.SemaphoreType.DMA((RN,)),
        ],
        compiler_params=params(0),
        cost_estimate=heavy(),
        name="pointwise",
    )(parts, bias.reshape(1, -1), bias_two.reshape(1, -1))


def back_kernel(share, where, grads, up, up_two, out, rows, held, total, made, sems):
    width, units = up.shape
    tile = width // 3
    parts = [slice(t * tile, (t + 1) * tile) for t in range(3)]
    z, x = where[0], where[1]
    first = len(BLOCKS)
    loads, fetches, sends = [], [], []
    for i, (side, k) in enumerate(BLOCKS):
        owner = lax.rem(z + k + ZN, ZN) + ZN * (1 - x if side else x)
        at = pl.multiple_of(owner * share, share)
        source = grads.at[i * share : (i + 1) * share, : 2 * units]
        loads.append(pltpu.make_async_copy(source, rows.at[pl.ds(at, share), :], sems.at[i]))
    for t, part in enumerate(parts):
        fetches.append(
            pltpu.make_async_copy(up_two.at[part, :], held.at[part, :], sems.at[first + t])
        )
    for copy in loads + fetches:
        copy.start()
    for copy in loads:
        copy.wait()
    for part in parts:
        total[:, part] = dot_t(rows[:, :units], up[part, :])
    for t, part in enumerate(parts):
        fetches[t].wait()
        made[:, part] = (total[:, part] + dot_t(rows[:, units:], held[part, :])).astype(BF16)
        sends.append(
            pltpu.make_async_copy(made.at[:, part], out.at[:, part], sems.at[first + 3 + t])
        )
        sends[-1].start()
    for copy in sends:
        copy.wait()


def back(where, both, up, up_two, share):
    width, units = up.shape
    count = both.shape[0]
    return pl.pallas_call(
        functools.partial(back_kernel, share),
        out_shape=pltpu.HBM((count, width), BF16),
        in_specs=[pl.BlockSpec(memory_space=pltpu.SMEM), REMAIN, WHOLE, FAR],
        out_specs=FAR,
        scratch_shapes=[
            pltpu.VMEM((count, 2 * units), BF16),
            pltpu.VMEM(up.shape, BF16),
            pltpu.VMEM((count, width), F32),
            pltpu.VMEM((count, width), BF16),
            pltpu.SemaphoreType.DMA((len(BLOCKS) + 6,)),
        ],
        compiler_params=params(0),
        cost_estimate=light(),
        name="back",
    )(where, both, up, in_hbm(up_two))


def collect_kernel(parts, out, held, sems):
    count = out.shape[0]
    loads = []
    for r in range(4):
        at = slice(r * held.shape[0] // 4, (r + 1) * held.shape[0] // 4)
        loads.append(pltpu.make_async_copy(parts.at[at, :], held.at[at, :], sems.at[r]))
    for copy in loads:
        copy.start()
    sums = jnp.zeros(out.shape, F32)
    for r in range(held.shape[0] // count):
        if r * count % (held.shape[0] // 4) == 0:
            loads[r * count // (held.shape[0] // 4)].wait()
        sums += held[r * count : (r + 1) * count, :].astype(F32)
    out[...] = sums.astype(BF16)


def collect(parts, share):
    return pl.pallas_call(
        collect_kernel,
        out_shape=jax.ShapeDtypeStruct((share, parts.shape[1]), BF16),
        in_specs=[REMAIN],
        out_specs=WHOLE,
        scratch_shapes=[pltpu.VMEM(parts.shape, BF16), pltpu.SemaphoreType.DMA((4,))],
        compiler_params=params(0),
        cost_estimate=light(),
        name="collect",
    )(parts)


def outer_kernel(factor, left, left_two, right, right_two, out):
    sums = dot_rows(left[...], right[...]) + dot_rows(left_two[...], right_two[...])
    out[...] = (sums * factor).astype(BF16)


def outer(factor, tiles, left, left_two, right, right_two):
    count = left[0].shape[0]
    size = left[2] // tiles

    def tiled(given):
        array, first, columns = given
        return pl.BlockSpec((count, size), lambda j: (0, first * tiles + j))

    def full(given):
        array, first, columns = given
        return pl.BlockSpec((count, columns), lambda j: (0, first))

    return pl.pallas_call(
        functools.partial(outer_kernel, factor),
        grid=(tiles,),
        out_shape=jax.ShapeDtypeStruct((left[2], right[2]), BF16),
        in_specs=[tiled(left), tiled(left_two), full(right), full(right_two)],
        out_specs=pl.BlockSpec((size, right[2]), lambda j: (j, 0)),
        compiler_params=params(1),
        cost_estimate=light(),
        name="outer",
    )(left[0], left_two[0], right[0], right_two[0])


def on_device(tokens, up_weight, up_bias, down_weight, cotangent):
    width, units = up_weight.shape
    share = tokens.shape[0]
    where = jnp.stack([lax.axis_index("z"), lax.axis_index("x_lo")]).astype(jnp.int32)

    held = pack(tokens, cotangent)
    across = swap(held, "x_lo")
    forward = jnp.concatenate([held, across], axis=0)
    backward = held
    fore, aft = [], []
    for k in range(1, ZN // 2 + 1):
        backward = shift_z(backward, -1)
        if k < ZN // 2:
            forward = shift_z(forward, 1)
            fore.append(forward)
        aft += [backward, swap(backward, "x_lo")]
    pieces = [held, across] + fore + aft

    up_two, down_two, bias_two = (swap(w, "core") for w in (up_weight, down_weight, up_bias))
    parts, rows = project(pieces, up_weight, up_two, down_weight, down_two)
    parts = lax.all_to_all(parts, ROW, 0, 0, tiled=True)
    both = pointwise(parts, up_bias, bias_two)
    both = lax.all_to_all(both, ROW, 0, 0, tiled=True)

    near = back(where, both, up_weight, up_two, share)
    near = lax.all_to_all(near, ("x_lo", "z"), 0, 0, tiled=True)
    grad_tokens = collect(near, share)

    rows_two = swap(rows, "core")
    both_two = swap(both[:, units : 3 * units], "core")
    factor = 1.0 / math.sqrt(2 * rows.shape[0])
    grad_up = outer(
        factor, 3, (rows, 0, width), (rows_two, 0, width), (both, 0, units), (both_two, 0, units)
    )
    grad_down = outer(
        factor, 3, (both, 3, units), (both_two, 1, units), (rows, 1, width), (rows_two, 1, width)
    )
    return (grad_tokens, grad_up, grad_down)


def solution(mesh):
    fine = Mesh(mesh.devices.reshape(4, 2, 2, 8, 2), ROW + COL)
    placed = (P(COL, ROW), P(ROW, COL), P(COL), P(COL, ROW), P(COL, ROW))
    return jax.shard_map(
        on_device,
        mesh=fine,
        in_specs=placed,
        out_specs=(P(COL, ROW), P(ROW, COL), P(COL, ROW)),
        check_vma=False,
    )
```

```python
import functools
import math

import jax
import jax.numpy as jnp
from jax import lax
from jax.experimental import pallas as pl
from jax.experimental.pallas import tpu as pltpu
from jax.sharding import Mesh, PartitionSpec as P

ROW = ("y", "x_hi")
COL = ("x_lo", "z", "core")
BF16 = jnp.bfloat16
F32 = jnp.float32
ZN = 8
RN = 8
BLOCKS = tuple((side, k) for k in (0, -1, -2, -3, 1, 2, 3, 4) for side in (0, 1))
WHOLE = pl.BlockSpec(memory_space=pltpu.VMEM)
REMAIN = pl.BlockSpec(memory_space=pl.ANY)
FAR = pl.BlockSpec(memory_space=pltpu.HBM)


def in_hbm(x):
    return pltpu.with_memory_space_constraint(x, pltpu.HBM)


def in_vmem(x):
    return pltpu.with_memory_space_constraint(x, pltpu.VMEM)


def light():
    return pl.CostEstimate(flops=1, bytes_accessed=1, transcendentals=0)


def heavy():
    return pl.CostEstimate(flops=2 * 10**10, bytes_accessed=2 * 10**6, transcendentals=0)


def params(steps):
    return pltpu.CompilerParams(
        dimension_semantics=("arbitrary",) * steps, vmem_limit_bytes=20 * 2**20
    )


def gelu_value(hidden):
    return hidden * 0.5 * (1.0 + lax.erf(hidden / math.sqrt(2.0)))


def gelu_slope(hidden):
    cumulative = 0.5 * (1.0 + lax.erf(hidden / math.sqrt(2.0)))
    density = jnp.exp(-0.5 * hidden * hidden) / math.sqrt(2.0 * math.pi)
    return cumulative + hidden * density


def shift_z(x, k):
    return lax.ppermute(x, "z", [(i, (i + k) % ZN) for i in range(ZN)])


def swap(x, axis):
    return lax.ppermute(x, axis, [(0, 1), (1, 0)])


def dot(a, b):
    return jnp.dot(a, b, preferred_element_type=F32)


def dot_t(a, b):
    return lax.dot_general(a, b, (((1,), (1,)), ((), ())), preferred_element_type=F32)


def dot_rows(a, b):
    return lax.dot_general(a, b, (((0,), (0,)), ((), ())), preferred_element_type=F32)


def pack_kernel(tokens, cotangent, out, sems):
    width = tokens.shape[1]
    copies = [
        pltpu.make_async_copy(tokens, out.at[:, :width], sems.at[0]),
        pltpu.make_async_copy(cotangent, out.at[:, width:], sems.at[1]),
    ]
    for copy in copies:
        copy.start()
    for copy in copies:
        copy.wait()


def pack(tokens, cotangent):
    return pl.pallas_call(
        pack_kernel,
        out_shape=jax.ShapeDtypeStruct((tokens.shape[0], 2 * tokens.shape[1]), BF16),
        in_specs=[FAR] * 2,
        out_specs=REMAIN,
        scratch_shapes=[pltpu.SemaphoreType.DMA((2,))],
        compiler_params=params(0),
        cost_estimate=heavy(),
        name="pack",
    )(in_hbm(tokens), in_hbm(cotangent))


def project_kernel(pieces, width, units, *refs):
    given, weights = refs[:pieces], refs[pieces : pieces + 4]
    out, kept, rows, made, sems = refs[pieces + 4 :]
    loads, base = [], 0
    for piece in given:
        at = rows.at[base : base + piece.shape[0], :]
        loads.append(pltpu.make_async_copy(piece, at, sems.at[len(loads)]))
        base += piece.shape[0]
    for copy in loads:
        copy.start()
    for copy in loads:
        copy.wait()
    sends = [
        pltpu.make_async_copy(rows, kept, sems.at[pieces]),
    ]
    for copy in sends:
        copy.start()
    for k, weight in enumerate(weights):
        at = slice(k * units, (k + 1) * units)
        if k < 2:
            product = dot(rows[:, :width], weight[...])
        else:
            product = dot_t(rows[:, width:], weight[...])
        made[:, at] = product.astype(BF16)
        sends.append(
            pltpu.make_async_copy(made.at[:, at], out.at[:, at], sems.at[pieces + 1 + k])
        )
        sends[-1].start()
    for copy in sends:
        copy.wait()


def project(pieces, up, up_two, down, down_two):
    width, units = up.shape
    count = sum(piece.shape[0] for piece in pieces)
    return pl.pallas_call(
        functools.partial(project_kernel, len(pieces), width, units),
        out_shape=[
            pltpu.HBM((count, 4 * units), BF16),
            jax.ShapeDtypeStruct((count, 2 * width), BF16),
        ],
        in_specs=[REMAIN] * len(pieces) + [WHOLE] * 4,
        out_specs=[FAR, REMAIN],
        scratch_shapes=[
            pltpu.VMEM((count, 2 * width), BF16),
            pltpu.VMEM((count, 4 * units), BF16),
            pltpu.SemaphoreType.DMA((len(pieces) + 5,)),
        ],
        compiler_params=params(0),
        cost_estimate=light(),
        name="project",
    )(*pieces, up, up_two, down, down_two)


def pointwise_kernel(parts, bias, bias_two, out, made, sems):
    count = parts.shape[0] // RN
    units = parts.shape[1] // 4
    for k, offset in enumerate((bias, bias_two)):
        hidden = offset[...].astype(F32) + jnp.zeros((count, units), F32)
        act_grad = jnp.zeros((count, units), F32)
        for r in range(RN):
            some = parts[r * count : (r + 1) * count, :]
            hidden += some[:, k * units : (k + 1) * units].astype(F32)
            act_grad += some[:, (2 + k) * units : (3 + k) * units].astype(F32)
        activated = gelu_value(hidden).astype(BF16)
        hidden_grad = (act_grad * gelu_slope(hidden)).astype(BF16)
        at = (3 - k) * units
        made[:, k * units : (k + 1) * units] = hidden_grad
        made[:, at : at + units] = activated
    sends = [
        pltpu.make_async_copy(made, out.at[r * count : (r + 1) * count, :], sems.at[r])
        for r in range(RN)
    ]
    for send in sends:
        send.start()
    for send in sends:
        send.wait()


def pointwise(parts, bias, bias_two):
    return pl.pallas_call(
        pointwise_kernel,
        out_shape=pltpu.HBM(parts.shape, BF16),
        in_specs=[WHOLE] * 3,
        out_specs=FAR,
        scratch_shapes=[
            pltpu.VMEM((parts.shape[0] // RN, parts.shape[1]), BF16),
            pltpu.SemaphoreType.DMA((RN,)),
        ],
        compiler_params=params(0),
        cost_estimate=heavy(),
        name="pointwise",
    )(parts, bias.reshape(1, -1), bias_two.reshape(1, -1))


def back_kernel(share, where, grads, up, up_two, out, rows, held, held_two, total, made, sems):
    width, units = up.shape
    tile = width // 3
    parts = [slice(t * tile, (t + 1) * tile) for t in range(3)]
    z, x = where[0], where[1]
    first = len(BLOCKS)
    loads, fetches, sends = [], [], []
    for i, (side, k) in enumerate(BLOCKS):
        owner = lax.rem(z + k + ZN, ZN) + ZN * (1 - x if side else x)
        at = pl.multiple_of(owner * share, share)
        source = grads.at[i * share : (i + 1) * share, : 2 * units]
        loads.append(pltpu.make_async_copy(source, rows.at[pl.ds(at, share), :], sems.at[i]))
    for weight, place in ((up, held), (up_two, held_two)):
        for part in parts:
            sem = sems.at[first + len(fetches)]
            fetches.append(pltpu.make_async_copy(weight.at[part, :], place.at[part, :], sem))
    for copy in loads + fetches[:4]:
        copy.start()
    for copy in loads:
        copy.wait()
    for t, fetch in enumerate(fetches):
        part = parts[t % 3]
        fetch.wait()
        if t + 4 < len(fetches):
            fetches[t + 4].start()
        if t < 3:
            total[:, part] = dot_t(rows[:, :units], held[part, :])
        else:
            sums = total[:, part] + dot_t(rows[:, units:], held_two[part, :])
            made[:, part] = sums.astype(BF16)
            sem = sems.at[first + 3 + t]
            sends.append(pltpu.make_async_copy(made.at[:, part], out.at[:, part], sem))
            sends[-1].start()
    for copy in sends:
        copy.wait()


def back(where, both, up, up_two, share):
    width, units = up.shape
    count = both.shape[0]
    return pl.pallas_call(
        functools.partial(back_kernel, share),
        out_shape=pltpu.HBM((count, width), BF16),
        in_specs=[pl.BlockSpec(memory_space=pltpu.SMEM), REMAIN, FAR, FAR],
        out_specs=FAR,
        scratch_shapes=[
            pltpu.VMEM((count, 2 * units), BF16),
            pltpu.VMEM(up.shape, BF16),
            pltpu.VMEM(up.shape, BF16),
            pltpu.VMEM((count, width), F32),
            pltpu.VMEM((count, width), BF16),
            pltpu.SemaphoreType.DMA((len(BLOCKS) + 9,)),
        ],
        compiler_params=params(0),
        cost_estimate=light(),
        name="back",
    )(where, both, in_hbm(up), in_hbm(up_two))


def collect_kernel(parts, out, held, sems):
    count = out.shape[0]
    loads = []
    for r in range(4):
        at = slice(r * held.shape[0] // 4, (r + 1) * held.shape[0] // 4)
        loads.append(pltpu.make_async_copy(parts.at[at, :], held.at[at, :], sems.at[r]))
    for copy in loads:
        copy.start()
    sums = jnp.zeros(out.shape, F32)
    for r in range(held.shape[0] // count):
        if r * count % (held.shape[0] // 4) == 0:
            loads[r * count // (held.shape[0] // 4)].wait()
        sums += held[r * count : (r + 1) * count, :].astype(F32)
    out[...] = sums.astype(BF16)


def collect(parts, share):
    return pl.pallas_call(
        collect_kernel,
        out_shape=jax.ShapeDtypeStruct((share, parts.shape[1]), BF16),
        in_specs=[REMAIN],
        out_specs=WHOLE,
        scratch_shapes=[pltpu.VMEM(parts.shape, BF16), pltpu.SemaphoreType.DMA((4,))],
        compiler_params=params(0),
        cost_estimate=light(),
        name="collect",
    )(parts)


def outer_kernel(factor, left, left_two, right, right_two, out):
    sums = dot_rows(left[...], right[...]) + dot_rows(left_two[...], right_two[...])
    out[...] = (sums * factor).astype(BF16)


def outer(factor, tiles, left, left_two, right, right_two):
    count = left[0].shape[0]
    size = left[2] // tiles

    def tiled(given):
        array, first, columns = given
        return pl.BlockSpec((count, size), lambda j: (0, first * tiles + j))

    def full(given):
        array, first, columns = given
        return pl.BlockSpec((count, columns), lambda j: (0, first))

    return pl.pallas_call(
        functools.partial(outer_kernel, factor),
        grid=(tiles,),
        out_shape=jax.ShapeDtypeStruct((left[2], right[2]), BF16),
        in_specs=[tiled(left), tiled(left_two), full(right), full(right_two)],
        out_specs=pl.BlockSpec((size, right[2]), lambda j: (j, 0)),
        compiler_params=params(1),
        cost_estimate=light(),
        name="outer",
    )(left[0], left_two[0], right[0], right_two[0])


def on_device(tokens, up_weight, up_bias, down_weight, cotangent):
    width, units = up_weight.shape
    share = tokens.shape[0]
    where = jnp.stack([lax.axis_index("z"), lax.axis_index("x_lo")]).astype(jnp.int32)

    held = pack(tokens, cotangent)
    across = swap(held, "x_lo")
    forward = jnp.concatenate([held, across], axis=0)
    backward = held
    fore, aft = [], []
    for k in range(1, ZN // 2 + 1):
        backward = shift_z(backward, -1)
        if k < ZN // 2:
            forward = shift_z(forward, 1)
            fore.append(forward)
        aft += [backward, swap(backward, "x_lo")]
    pieces = [held, across] + fore + aft

    up_two, down_two, bias_two = (swap(w, "core") for w in (up_weight, down_weight, up_bias))
    parts, rows = project(pieces, up_weight, up_two, down_weight, down_two)
    parts = lax.all_to_all(parts, ROW, 0, 0, tiled=True)
    both = pointwise(parts, up_bias, bias_two)
    both = lax.all_to_all(both, ROW, 0, 0, tiled=True)

    near = back(where, both, up_weight, up_two, share)
    near = lax.all_to_all(near, ("x_lo", "z"), 0, 0, tiled=True)
    grad_tokens = collect(near, share)

    rows_two = swap(rows, "core")
    both_two = swap(both[:, units : 3 * units], "core")
    factor = 1.0 / math.sqrt(2 * rows.shape[0])
    grad_up = outer(
        factor, 3, (rows, 0, width), (rows_two, 0, width), (both, 0, units), (both_two, 0, units)
    )
    grad_down = outer(
        factor, 3, (both, 3, units), (both_two, 1, units), (rows, 1, width), (rows_two, 1, width)
    )
    return (grad_tokens, grad_up, grad_down)


def solution(mesh):
    fine = Mesh(mesh.devices.reshape(4, 2, 2, 8, 2), ROW + COL)
    placed = (P(COL, ROW), P(ROW, COL), P(COL), P(COL, ROW), P(COL, ROW))
    return jax.shard_map(
        on_device,
        mesh=fine,
        in_specs=placed,
        out_specs=(P(COL, ROW), P(ROW, COL), P(COL, ROW)),
        check_vma=False,
    )
```

```python
import functools
import math

import jax
import jax.numpy as jnp
from jax import lax
from jax.experimental import pallas as pl
from jax.experimental.pallas import tpu as pltpu
from jax.sharding import Mesh, PartitionSpec as P

ROW = ("y", "x_hi")
COL = ("x_lo", "z", "core")
BF16 = jnp.bfloat16
F32 = jnp.float32
ZN = 8
RN = 8
BLOCKS = tuple((side, k) for k in (0, -1, -2, -3, 1, 2, 3, 4) for side in (0, 1))
WHOLE = pl.BlockSpec(memory_space=pltpu.VMEM)
REMAIN = pl.BlockSpec(memory_space=pl.ANY)
FAR = pl.BlockSpec(memory_space=pltpu.HBM)


def in_hbm(x):
    return pltpu.with_memory_space_constraint(x, pltpu.HBM)


def in_vmem(x):
    return pltpu.with_memory_space_constraint(x, pltpu.VMEM)


def light():
    return pl.CostEstimate(flops=1, bytes_accessed=1, transcendentals=0)


def heavy():
    return pl.CostEstimate(flops=2 * 10**10, bytes_accessed=2 * 10**6, transcendentals=0)


def params(steps):
    return pltpu.CompilerParams(
        dimension_semantics=("arbitrary",) * steps, vmem_limit_bytes=20 * 2**20
    )


def gelu_value(hidden):
    return hidden * 0.5 * (1.0 + lax.erf(hidden / math.sqrt(2.0)))


def gelu_slope(hidden):
    cumulative = 0.5 * (1.0 + lax.erf(hidden / math.sqrt(2.0)))
    density = jnp.exp(-0.5 * hidden * hidden) / math.sqrt(2.0 * math.pi)
    return cumulative + hidden * density


def shift_z(x, k):
    return lax.ppermute(x, "z", [(i, (i + k) % ZN) for i in range(ZN)])


def swap(x, axis):
    return lax.ppermute(x, axis, [(0, 1), (1, 0)])


def dot(a, b):
    return jnp.dot(a, b, preferred_element_type=F32)


def dot_t(a, b):
    return lax.dot_general(a, b, (((1,), (1,)), ((), ())), preferred_element_type=F32)


def dot_rows(a, b):
    return lax.dot_general(a, b, (((0,), (0,)), ((), ())), preferred_element_type=F32)


def pack_kernel(tokens, cotangent, out, sems):
    width = tokens.shape[1]
    copies = [
        pltpu.make_async_copy(tokens, out.at[:, :width], sems.at[0]),
        pltpu.make_async_copy(cotangent, out.at[:, width:], sems.at[1]),
    ]
    for copy in copies:
        copy.start()
    for copy in copies:
        copy.wait()


def pack(tokens, cotangent):
    return pl.pallas_call(
        pack_kernel,
        out_shape=jax.ShapeDtypeStruct((tokens.shape[0], 2 * tokens.shape[1]), BF16),
        in_specs=[FAR] * 2,
        out_specs=REMAIN,
        scratch_shapes=[pltpu.SemaphoreType.DMA((2,))],
        compiler_params=params(0),
        cost_estimate=heavy(),
        name="pack",
    )(in_hbm(tokens), in_hbm(cotangent))


def project_kernel(pieces, width, units, *refs):
    given, weights = refs[:pieces], refs[pieces : pieces + 4]
    out, kept, rows, made, sems = refs[pieces + 4 :]
    loads, base = [], 0
    for piece in given:
        at = rows.at[base : base + piece.shape[0], :]
        loads.append(pltpu.make_async_copy(piece, at, sems.at[len(loads)]))
        base += piece.shape[0]
    for copy in loads:
        copy.start()
    for copy in loads:
        copy.wait()
    sends = [
        pltpu.make_async_copy(rows, kept, sems.at[pieces]),
    ]
    for copy in sends:
        copy.start()
    for k, weight in enumerate(weights):
        at = slice(k * units, (k + 1) * units)
        if k < 2:
            product = dot(rows[:, :width], weight[...])
        else:
            product = dot_t(rows[:, width:], weight[...])
        made[:, at] = product.astype(BF16)
        sends.append(
            pltpu.make_async_copy(made.at[:, at], out.at[:, at], sems.at[pieces + 1 + k])
        )
        sends[-1].start()
    for copy in sends:
        copy.wait()


def project(pieces, up, up_two, down, down_two):
    width, units = up.shape
    count = sum(piece.shape[0] for piece in pieces)
    return pl.pallas_call(
        functools.partial(project_kernel, len(pieces), width, units),
        out_shape=[
            pltpu.HBM((count, 4 * units), BF16),
            jax.ShapeDtypeStruct((count, 2 * width), BF16),
        ],
        in_specs=[REMAIN] * len(pieces) + [WHOLE] * 4,
        out_specs=[FAR, REMAIN],
        scratch_shapes=[
            pltpu.VMEM((count, 2 * width), BF16),
            pltpu.VMEM((count, 4 * units), BF16),
            pltpu.SemaphoreType.DMA((len(pieces) + 5,)),
        ],
        compiler_params=params(0),
        cost_estimate=light(),
        name="project",
    )(*pieces, up, up_two, down, down_two)


def pointwise_kernel(parts, bias, bias_two, out, made, sems):
    count = parts.shape[0] // RN
    units = parts.shape[1] // 4
    for k, offset in enumerate((bias, bias_two)):
        hidden = offset[...].astype(F32) + jnp.zeros((count, units), F32)
        act_grad = jnp.zeros((count, units), F32)
        for r in range(RN):
            some = parts[r * count : (r + 1) * count, :]
            hidden += some[:, k * units : (k + 1) * units].astype(F32)
            act_grad += some[:, (2 + k) * units : (3 + k) * units].astype(F32)
        activated = gelu_value(hidden).astype(BF16)
        hidden_grad = (act_grad * gelu_slope(hidden)).astype(BF16)
        at = (3 - k) * units
        made[:, k * units : (k + 1) * units] = hidden_grad
        made[:, at : at + units] = activated
    sends = [
        pltpu.make_async_copy(made, out.at[r * count : (r + 1) * count, :], sems.at[r])
        for r in range(RN)
    ]
    for send in sends:
        send.start()
    for send in sends:
        send.wait()


def pointwise(parts, bias, bias_two):
    return pl.pallas_call(
        pointwise_kernel,
        out_shape=pltpu.HBM(parts.shape, BF16),
        in_specs=[WHOLE] * 3,
        out_specs=FAR,
        scratch_shapes=[
            pltpu.VMEM((parts.shape[0] // RN, parts.shape[1]), BF16),
            pltpu.SemaphoreType.DMA((RN,)),
        ],
        compiler_params=params(0),
        cost_estimate=heavy(),
        name="pointwise",
    )(parts, bias.reshape(1, -1), bias_two.reshape(1, -1))


def back_kernel(share, where, grads, up, up_two, out, rows, held, held_two, total, made, sems):
    width, units = up.shape
    tile = width // 3
    parts = [slice(t * tile, (t + 1) * tile) for t in range(3)]
    z, x = where[0], where[1]
    first = len(BLOCKS)
    loads, fetches, sends = [], [], []
    for i, (side, k) in enumerate(BLOCKS):
        owner = lax.rem(z + k + ZN, ZN) + ZN * (1 - x if side else x)
        at = pl.multiple_of(owner * share, share)
        source = grads.at[i * share : (i + 1) * share, : 2 * units]
        loads.append(pltpu.make_async_copy(source, rows.at[pl.ds(at, share), :], sems.at[i]))
    for weight, place in ((up, held), (up_two, held_two)):
        for part in parts:
            sem = sems.at[first + len(fetches)]
            fetches.append(pltpu.make_async_copy(weight.at[part, :], place.at[part, :], sem))
    for copy in loads + fetches:
        copy.start()
    for copy in loads:
        copy.wait()
    for t, fetch in enumerate(fetches):
        part = parts[t % 3]
        fetch.wait()
        if t < 3:
            total[:, part] = dot_t(rows[:, :units], held[part, :])
        else:
            sums = total[:, part] + dot_t(rows[:, units:], held_two[part, :])
            made[:, part] = sums.astype(BF16)
            sem = sems.at[first + 3 + t]
            sends.append(pltpu.make_async_copy(made.at[:, part], out.at[:, part], sem))
            sends[-1].start()
    for copy in sends:
        copy.wait()


def back(where, both, up, up_two, share):
    width, units = up.shape
    count = both.shape[0]
    return pl.pallas_call(
        functools.partial(back_kernel, share),
        out_shape=pltpu.HBM((count, width), BF16),
        in_specs=[pl.BlockSpec(memory_space=pltpu.SMEM), REMAIN, FAR, FAR],
        out_specs=FAR,
        scratch_shapes=[
            pltpu.VMEM((count, 2 * units), BF16),
            pltpu.VMEM(up.shape, BF16),
            pltpu.VMEM(up.shape, BF16),
            pltpu.VMEM((count, width), F32),
            pltpu.VMEM((count, width), BF16),
            pltpu.SemaphoreType.DMA((len(BLOCKS) + 9,)),
        ],
        compiler_params=params(0),
        cost_estimate=light(),
        name="back",
    )(where, both, in_hbm(up), in_hbm(up_two))


def collect_kernel(parts, out, held, sems):
    count = out.shape[0]
    loads = []
    for r in range(4):
        at = slice(r * held.shape[0] // 4, (r + 1) * held.shape[0] // 4)
        loads.append(pltpu.make_async_copy(parts.at[at, :], held.at[at, :], sems.at[r]))
    for copy in loads:
        copy.start()
    sums = jnp.zeros(out.shape, F32)
    for r in range(held.shape[0] // count):
        if r * count % (held.shape[0] // 4) == 0:
            loads[r * count // (held.shape[0] // 4)].wait()
        sums += held[r * count : (r + 1) * count, :].astype(F32)
    out[...] = sums.astype(BF16)


def collect(parts, share):
    return pl.pallas_call(
        collect_kernel,
        out_shape=jax.ShapeDtypeStruct((share, parts.shape[1]), BF16),
        in_specs=[REMAIN],
        out_specs=WHOLE,
        scratch_shapes=[pltpu.VMEM(parts.shape, BF16), pltpu.SemaphoreType.DMA((4,))],
        compiler_params=params(0),
        cost_estimate=light(),
        name="collect",
    )(parts)


def outer_kernel(factor, left, left_two, right, right_two, out):
    sums = dot_rows(left[...], right[...]) + dot_rows(left_two[...], right_two[...])
    out[...] = (sums * factor).astype(BF16)


def outer(factor, tiles, left, left_two, right, right_two):
    count = left[0].shape[0]
    size = left[2] // tiles

    def tiled(given):
        array, first, columns = given
        return pl.BlockSpec((count, size), lambda j: (0, first * tiles + j))

    def full(given):
        array, first, columns = given
        return pl.BlockSpec((count, columns), lambda j: (0, first))

    return pl.pallas_call(
        functools.partial(outer_kernel, factor),
        grid=(tiles,),
        out_shape=jax.ShapeDtypeStruct((left[2], right[2]), BF16),
        in_specs=[tiled(left), tiled(left_two), full(right), full(right_two)],
        out_specs=pl.BlockSpec((size, right[2]), lambda j: (j, 0)),
        compiler_params=params(1),
        cost_estimate=light(),
        name="outer",
    )(left[0], left_two[0], right[0], right_two[0])


def on_device(tokens, up_weight, up_bias, down_weight, cotangent):
    width, units = up_weight.shape
    share = tokens.shape[0]
    where = jnp.stack([lax.axis_index("z"), lax.axis_index("x_lo")]).astype(jnp.int32)

    held = pack(tokens, cotangent)
    across = swap(held, "x_lo")
    forward = jnp.concatenate([held, across], axis=0)
    backward = held
    fore, aft = [], []
    for k in range(1, ZN // 2 + 1):
        backward = shift_z(backward, -1)
        if k < ZN // 2:
            forward = shift_z(forward, 1)
            fore.append(forward)
        aft += [backward, swap(backward, "x_lo")]
    pieces = [held, across] + fore + aft

    up_two, down_two, bias_two = (swap(w, "core") for w in (up_weight, down_weight, up_bias))
    parts, rows = project(pieces, up_weight, up_two, down_weight, down_two)
    parts = lax.all_to_all(parts, ROW, 0, 0, tiled=True)
    both = pointwise(parts, up_bias, bias_two)
    both = lax.all_to_all(both, ROW, 0, 0, tiled=True)

    near = back(where, both, up_weight, up_two, share)
    near = lax.all_to_all(near, ("x_lo", "z"), 0, 0, tiled=True)
    grad_tokens = collect(near, share)

    rows_two = swap(rows, "core")
    both_two = swap(both[:, units : 3 * units], "core")
    factor = 1.0 / math.sqrt(2 * rows.shape[0])
    grad_up = outer(
        factor, 3, (rows, 0, width), (rows_two, 0, width), (both, 0, units), (both_two, 0, units)
    )
    grad_down = outer(
        factor, 3, (both, 3, units), (both_two, 1, units), (rows, 1, width), (rows_two, 1, width)
    )
    return (grad_tokens, grad_up, grad_down)


def solution(mesh):
    fine = Mesh(mesh.devices.reshape(4, 2, 2, 8, 2), ROW + COL)
    placed = (P(COL, ROW), P(ROW, COL), P(COL), P(COL, ROW), P(COL, ROW))
    return jax.shard_map(
        on_device,
        mesh=fine,
        in_specs=placed,
        out_specs=(P(COL, ROW), P(ROW, COL), P(COL, ROW)),
        check_vma=False,
    )
```
